32 devices in a mesh: groups: 2 (over x), tensor: 16 (over z, y, core).
Axes of the slice: x: 2, y: 2, z: 4, core: 2. Of those that a mesh axis runs over, the one named last changes fastest.
Arguments:
- hidden_in: bfloat16 [512, 5120], P(('groups', 'tensor')), parts along dimension 0, may hold values from -6 to 6
- norm_gain: float32 [5120], replicated, may hold values from 0.1 to 1.9
- w_gate: bfloat16 [5120, 17408], P(None, 'tensor'), may hold values from -0.078125 to 0.078125
- w_up: bfloat16 [5120, 17408], P(None, 'tensor'), may hold values from -0.078125 to 0.078125
- w_down: bfloat16 [17408, 5120], P('tensor'), may hold values from -0.046875 to 0.046875
- final_gain: float32 [5120], replicated, may hold values from 0.1 to 1.9
- adapter: bfloat16 [5120, 768], P('tensor'), may hold values from -0.078125 to 0.078125
- student_rows: bfloat16 [128, 768], P(('groups', 'tensor')), parts along dimension 0, may hold values from -6 to 6
- queries: float32 [32, 768], P(('groups', 'tensor')), parts along dimension 0, may hold values from -6 to 6
- doc_list: int32 [128], P(('groups', 'tensor')), parts along dimension 0, may hold values from 0 to 15, as said below
- teacher_rank: int32 [128], P(('groups', 'tensor')), parts along dimension 0, may hold values from 0 to 15, as said below
Outputs:
- teacher_rows: bfloat16 [128, 5120], P(('groups', 'tensor')), parts along dimension 0
- grad_rows: float32 [128, 768], P(('groups', 'tensor')), parts along dimension 0
- grad_queries: float32 [32, 768], P(('groups', 'tensor')), parts along dimension 0
- list_losses: float32 [32], P(('groups', 'tensor')), parts along dimension 0
The draws below stay inside these ranges and needn't reach their ends.
There are 2 independent parts, one for each index of `groups`. The reference program is written for one: setup_inputs(seed, part) draws one part's arguments, and reference() takes and returns one part's arrays. A program takes and returns all parts, laid end to end along the dimension named above; an argument that names none is the same for every part. Nothing has to cross between parts.
Inputs may be any that keep to these rules, and one draw needn't show every extreme that they name: `doc_list`: every list holds 1 to 16 documents and one list exactly 16. `teacher_rank`: within each list the ranks of its documents are 0 to its length minus 1, each once.
All inputs are finite; a program needn't handle non-finite values.
Results may differ from the reference program's by a relative error of at most 0.0051.
Values may be sent and summed in bfloat16 or wider, within the bound.
A program may use at most 128 MiB of HBM per device.

```python
import math
import jax
import jax.numpy as jnp
from jax import lax

D = 5120
FF = 17408
SW = 768
SEQ = 4
DOC_DEV = 4
TOKENS = 256
DOCS = 64
LISTS = 16


def list_layout(key):
    key_jump, key_order, key_docs = jax.random.split(key, 3)
    index = jnp.arange(LISTS, dtype=jnp.int32)
    jumps = jax.random.randint(key_jump, (LISTS,), 0, DOC_DEV, dtype=jnp.int32)
    pair_first = jnp.clip(5 + 2 * ((index - 5) // 2), 0, LISTS - 1)
    pair_jump = jumps[pair_first]
    plus_side = (index >= 5) & ((index - 5) % 2 == 0) & (index + 1 < LISTS)
    minus_side = (index >= 5) & ((index - 5) % 2 == 1)
    middle = DOC_DEV + jnp.where(plus_side, pair_jump, 0) - jnp.where(minus_side, pair_jump, 0)
    length_values = jnp.where(index == 0, 4 * DOC_DEV, jnp.where(index < 5, DOC_DEV // 4, middle)).astype(jnp.int32)
    length_values = length_values[jax.random.permutation(key_order, LISTS)]
    ends = jnp.cumsum(length_values).astype(jnp.int32)
    starts = ends - length_values
    slots = jnp.arange(DOCS, dtype=jnp.int32)
    owner = jnp.sum((slots[:, None] >= ends[None, :]).astype(jnp.int32), axis=1).astype(jnp.int32)
    within = slots - starts[owner]
    placed = jax.random.permutation(key_docs, DOCS)
    doc_ids = jnp.zeros((DOCS,), jnp.int32).at[placed].set(owner)
    ranks = jnp.zeros((DOCS,), jnp.int32).at[placed].set(within)
    return (doc_ids, ranks)


def draw_doc_list(key, part):
    doc_ids, ranks = list_layout(key)
    return doc_ids


def draw_teacher_rank(key, part):
    doc_ids, ranks = list_layout(key)
    return ranks


def levels(stream_key, shape, shards, smallest, largest):
    factor_of, own = 1.0, jax.random.fold_in(stream_key, 6)
    for axis_at, shards_of in shards:
        heights = jnp.exp(jax.random.uniform(jax.random.fold_in(own, axis_at), (shards_of,), jnp.float32, smallest / len(shards), largest / len(shards)))
        factor_of = factor_of * jnp.repeat(heights, shape[axis_at] // shards_of).reshape([-1 if axis == axis_at else 1 for axis in range(len(shape))])
    return factor_of


def scatter_about(rng, shape, deviation, most, cuts=(), kind=jnp.bfloat16):
    level = levels(rng, shape, cuts, -0.22, 0.18) if cuts else 1.0
    entries = jax.random.normal(rng, shape, jnp.float32) * deviation * level
    return jnp.minimum(jnp.maximum(entries, -most), most).astype(kind)


def setup_inputs(seed: int = 0, part: int = 0) -> dict:
    keys = jax.random.split(jax.random.key(seed), 12)
    own_keys = jax.random.split(jax.random.fold_in(keys[11], part), 12)
    hidden_in = scatter_about(own_keys[0], (TOKENS, D), 1.0, 6.0, ((0, 16),))
    norm_gain = jnp.clip(1.0 + 0.18 * jax.random.normal(keys[1], (D,), jnp.float32), 0.1, 1.9)
    w_gate = scatter_about(keys[2], (D, FF), D ** -0.5, 0.078125, ((1, 16),))
    w_up = scatter_about(keys[3], (D, FF), D ** -0.5, 0.078125, ((1, 16),))
    w_down = scatter_about(keys[4], (FF, D), FF ** -0.5, 0.046875, ((0, 16),))
    final_gain = jnp.clip(1.0 + 0.18 * jax.random.normal(keys[5], (D,), jnp.float32), 0.1, 1.9)
    adapter = scatter_about(keys[6], (D, SW), D ** -0.5, 0.078125, ((0, 16),))
    student_rows = scatter_about(own_keys[7], (DOCS, SW), 1.0, 6.0, ((0, 16),))
    queries = scatter_about(own_keys[8], (LISTS, SW), 1.0, 6.0, ((0, 16),), jnp.float32)
    doc_list = draw_doc_list(jax.random.fold_in(jax.random.fold_in(keys[11], part), 71), part)
    teacher_rank = draw_teacher_rank(jax.random.fold_in(jax.random.fold_in(keys[11], part), 71), part)
    return {"hidden_in": hidden_in, "norm_gain": norm_gain, "w_gate": w_gate, "w_up": w_up, "w_down": w_down, "final_gain": final_gain, "adapter": adapter, "student_rows": student_rows, "queries": queries, "doc_list": doc_list, "teacher_rank": teacher_rank}


EPSILON = 1e-06
SOFTMAX_HEAT = 0.5

def list_losses_of(score_values, member, rank_f):
    pairwise_terms = jnp.dot(member, member.T, precision=lax.Precision.HIGHEST)
    pairwise_terms = pairwise_terms * (1.0 - jnp.eye(score_values.shape[0], dtype=score_values.dtype))
    outranked_count = pairwise_terms * jax.nn.sigmoid((score_values[None, :] - score_values[:, None]) / SOFTMAX_HEAT)
    approx_rank = 1.0 + lax.optimization_barrier(jnp.sum(outranked_count, axis=1))
    gains = 1.0 / jnp.log2(2.0 + rank_f)
    earned = jnp.dot(member.T, gains / jnp.log2(1.0 + approx_rank), precision=lax.Precision.HIGHEST)
    ideal = jnp.dot(member.T, gains * gains, precision=lax.Precision.HIGHEST)
    return 1.0 - earned / ideal

def reference(hidden_in, norm_gain, w_gate, w_up, w_down, final_gain, adapter, student_rows, queries, doc_list, teacher_rank):
    tokens_f = hidden_in.astype(jnp.float32)
    normed = (tokens_f * lax.rsqrt(lax.optimization_barrier(jnp.mean(tokens_f * tokens_f, axis=-1, keepdims=True)) + EPSILON) * norm_gain).astype(jnp.bfloat16)
    gate_out = jnp.dot(normed, w_gate, preferred_element_type=jnp.float32)
    up_out = jnp.dot(normed, w_up, preferred_element_type=jnp.float32)
    hidden = (jax.nn.silu(gate_out) * up_out).astype(jnp.bfloat16)
    mixed = jnp.dot(hidden, w_down, preferred_element_type=jnp.float32)
    pooled = (tokens_f + mixed).reshape(DOCS, SEQ, D).mean(axis=1)
    normed_rows = pooled * lax.rsqrt(lax.optimization_barrier(jnp.mean(pooled * pooled, axis=-1, keepdims=True)) + EPSILON) * final_gain
    teacher_rows = normed_rows.astype(jnp.bfloat16)
    target = jnp.dot(teacher_rows, adapter, preferred_element_type=jnp.float32)
    member = (doc_list[:, None] == jnp.arange(LISTS, dtype=jnp.int32)[None, :]).astype(jnp.float32)
    rank_f = teacher_rank.astype(jnp.float32)
    scale_root = math.sqrt(SW)

    def objective(rows_f, query_f):
        chosen = jnp.dot(member, query_f, precision=lax.Precision.HIGHEST)
        score_values = lax.optimization_barrier(jnp.sum(rows_f * chosen, axis=1)) / scale_root
        per_list = list_losses_of(score_values, member, rank_f)
        residual = rows_f - target
        return (SW * jnp.sum(per_list) + 0.5 * jnp.sum(residual * residual), per_list)
    (unused_total, per_list), gradients = jax.value_and_grad(objective, argnums=(0, 1), has_aux=True)(student_rows.astype(jnp.float32), queries)
    return (teacher_rows, gradients[0], gradients[1], per_list)
```

```python
import math

import jax
import jax.numpy as jnp
from jax import lax
from jax.experimental import pallas as pl
from jax.experimental.pallas import tpu as pltpu
from jax.sharding import PartitionSpec as P

SEQ = 4


EPSILON = 1e-06
SOFTMAX_HEAT = 0.5


def list_losses_of(score_values, member, rank_f):
    pairwise_terms = jnp.dot(member, member.T, precision=lax.Precision.HIGHEST)
    pairwise_terms = pairwise_terms * (
        1.0 - jnp.eye(score_values.shape[0], dtype=score_values.dtype)
    )
    outranked_count = pairwise_terms * jax.nn.sigmoid(
        (score_values[None, :] - score_values[:, None]) / SOFTMAX_HEAT
    )
    approx_rank = 1.0 + jnp.sum(outranked_count, axis=1)
    gains = 1.0 / jnp.log2(2.0 + rank_f)
    earned = jnp.dot(member.T, gains / jnp.log2(1.0 + approx_rank), precision=lax.Precision.HIGHEST)
    ideal = jnp.dot(member.T, gains * gains, precision=lax.Precision.HIGHEST)
    return 1.0 - earned / ideal


def local(
    hidden_in,
    norm_gain,
    w_gate,
    w_up,
    w_down,
    final_gain,
    adapter,
    student_rows,
    queries,
    doc_list,
    teacher_rank,
):
    list_entries = lax.axis_size("tensor")
    my_index = lax.axis_index("tensor")
    tokens_f = hidden_in.astype(jnp.float32)
    normed = (
        tokens_f
        * lax.rsqrt(jnp.mean(tokens_f * tokens_f, axis=-1, keepdims=True) + EPSILON)
        * norm_gain
    ).astype(jnp.bfloat16)
    shard_rows = lax.all_gather(normed, "tensor", axis=0, tiled=True)
    gate_out = jnp.dot(shard_rows, w_gate, preferred_element_type=jnp.float32)
    up_out = jnp.dot(shard_rows, w_up, preferred_element_type=jnp.float32)
    hidden = (jax.nn.silu(gate_out) * up_out).astype(jnp.bfloat16)
    doc_rows = hidden_in.shape[0] // SEQ
    mixed = jnp.dot(hidden, w_down, preferred_element_type=jnp.float32)
    pooled_mix = lax.psum_scatter(
        mixed.reshape(lax.axis_size("tensor") * doc_rows, SEQ, mixed.shape[1]).mean(axis=1),
        "tensor",
        scatter_dimension=0,
        tiled=True,
    )
    pooled = pooled_mix + tokens_f.reshape(doc_rows, SEQ, tokens_f.shape[1]).mean(axis=1)
    normed_rows = (
        pooled * lax.rsqrt(jnp.mean(pooled * pooled, axis=-1, keepdims=True) + EPSILON) * final_gain
    )
    teacher_rows = normed_rows.astype(jnp.bfloat16)
    student_width = adapter.shape[1]
    target = jnp.dot(
        teacher_rows,
        lax.all_gather(adapter, "tensor", axis=0, tiled=True),
        preferred_element_type=jnp.float32,
    )
    rows_f = student_rows.astype(jnp.float32)
    residual = rows_f - target
    scale_root = math.sqrt(student_width)
    list_ids = jnp.arange(list_entries, dtype=jnp.int32)
    own_member = doc_list[:, None] == list_ids[None, :]
    query_all = lax.all_gather(queries, "tensor", axis=0, tiled=True)
    own_onehot = own_member.astype(jnp.float32)
    chosen = jnp.dot(own_onehot, query_all, precision=lax.Precision.HIGHEST)
    own_scores = jnp.sum(rows_f * chosen, axis=1) / scale_root
    all_scores = lax.all_gather(own_scores, "tensor", axis=0, tiled=True)
    all_lists, all_ranks = (
        lax.all_gather(doc_list, "tensor", axis=0, tiled=True),
        lax.all_gather(teacher_rank, "tensor", axis=0, tiled=True),
    )
    member = (all_lists[:, None] == list_ids[None, :]).astype(jnp.float32)
    rank_f = all_ranks.astype(jnp.float32)
    per_list, pullback = jax.vjp(lambda values: list_losses_of(values, member, rank_f), all_scores)
    score_grad = pullback(jnp.full(per_list.shape, float(student_width), jnp.float32))[0]
    own_grad = lax.dynamic_slice_in_dim(score_grad, my_index * doc_rows, doc_rows, 0)
    grad_rows = own_grad[:, None] * chosen / scale_root + residual
    query_terms = (
        jnp.dot(own_onehot.T, own_grad[:, None] * rows_f, precision=lax.Precision.HIGHEST)
        / scale_root
    )
    grad_queries = lax.psum_scatter(query_terms, "tensor", scatter_dimension=0, tiled=True)
    own_losses = lax.dynamic_slice_in_dim(per_list, my_index, 1, 0)
    return (teacher_rows, grad_rows, grad_queries, own_losses)


CHIPS = 8
COLS = 640
HALF = 2560
FIRST = 160
F32 = jnp.float32
BF16 = jnp.bfloat16


def chip_at(pos):
    y = pos // 4
    return 2 * (pos + y * (7 - 2 * pos)) + y


def pos_of(chip):
    y = chip % 2
    z = chip // 2
    return z + y * (7 - 2 * z)


def slot_of(rel):
    return 2 * rel if rel < 4 else 15 - 2 * rel


def slot_vec(chip, p):
    y = chip & 1
    z = chip >> 1
    rel = (z + y * (7 - 2 * z) - p + 8) & 7
    return jnp.where(rel < 4, 2 * rel, 15 - 2 * rel)


def kernel(
    hin, ngain, wg_hbm, wu_hbm, wd_hbm, fgain, ad_hbm, student, query, lists, ranks,
    out_rows, out_grad, out_query, out_loss,
    xraw, xn, wg, wu, wd, ad, hid, part, sib_out, sib_in, rs_r_out, rs_r_in, rs_l_out, rs_l_in,
    fin_out, fin, small, gvec,
    w_sem, ag_rs, ag_rr, ag_ls, ag_lr, ag_ss, ag_sr, ad_sem, sm_s, sm_r, sms_s, sms_r,
    sb_s, sb_r, rr_s, rr_r, rl_s, rl_r, fi_s, fi_r,
):
    t = lax.axis_index("tensor")
    c = t % 2
    chip = t // 2
    p = pos_of(chip)

    def plane(rel):
        return chip_at((p + rel) % CHIPS) * 2 + c

    right, left, sibling = plane(1), plane(7), chip * 2 + (1 - c)
    sent = []

    def remote(src, dst, ssem, rsem, dev):
        return pltpu.make_async_remote_copy(
            src_ref=src, dst_ref=dst, send_sem=ssem, recv_sem=rsem,
            device_id={"tensor": dev}, device_id_type=pl.DeviceIdType.MESH,
        )

    def go(copy):
        copy.start()
        sent.append(copy)
        return copy

    barrier = pltpu.get_barrier_semaphore()
    for rel in range(1, CHIPS):
        pl.semaphore_signal(barrier, inc=1, device_id={"tensor": plane(rel)}, device_id_type=pl.DeviceIdType.MESH)
    pl.semaphore_signal(barrier, inc=1, device_id={"tensor": sibling}, device_id_type=pl.DeviceIdType.MESH)

    loads = []
    for i, (src, dst) in enumerate(((wg_hbm, wg), (wu_hbm, wu), (wd_hbm, wd))):
        rows = src.shape[0] // 4
        for j in range(4):
            copy = pltpu.make_async_copy(src.at[pl.ds(j * rows, rows)], dst.at[pl.ds(j * rows, rows)], w_sem.at[i, j])
            copy.start()
            loads.append(copy)
    ad_rows = pl.ds(pl.multiple_of(c * 320, 64), 320)
    ad_local = pltpu.make_async_copy(ad_hbm, ad.at[ad_rows], ad_sem.at[0])
    ad_local.start()
    pl.semaphore_wait(barrier, CHIPS)

    def block(slot, half):
        return pl.ds((slot * 2 + half) * 16, 16)

    def cols(h):
        return pl.ds(h * HALF, HALF)

    def hop(step, h, to_right):
        if to_right:
            src_slot = 0 if step == 0 else 2 * step - 1
            dst_slot = 2 * step + 1
            ssem, rsem, dev = ag_rs.at[step, h], ag_rr.at[step, h], right
        else:
            src_slot = 2 * step
            dst_slot = 2 * step + 2 if step < 3 else 7
            ssem, rsem, dev = ag_ls.at[step, h], ag_lr.at[step, h], left
        src = hin.at[:, cols(h)] if step == 0 else xraw.at[block(src_slot, 0), cols(h)]
        return remote(src, xraw.at[block(dst_slot, 0), cols(h)], ssem, rsem, dev)

    def share(slot, h):
        src = hin.at[:, cols(h)] if slot == 0 else xraw.at[block(slot, 0), cols(h)]
        return remote(src, xraw.at[block(slot, 1), cols(h)], ag_ss.at[slot, h], ag_sr.at[slot, h], sibling)

    hops = {}
    shares = {}
    for h in range(2):
        hops[0, h, True] = go(hop(0, h, True))
        hops[0, h, False] = go(hop(0, 1 - h, False))
    hops[0, 0, False], hops[0, 1, False] = hops[0, 1, False], hops[0, 0, False]
    for h in range(2):
        shares[0, h] = go(share(0, h))
    ad_remote = go(remote(ad_hbm, ad.at[ad_rows], ad_sem.at[1], ad_sem.at[2], sibling))

    small[0, 0:4, 0:768] = student[...].astype(F32)
    small[0, 4:5, 0:768] = query[...]
    row8 = lax.broadcasted_iota(jnp.int32, (8, 128), 0)
    lane8 = lax.broadcasted_iota(jnp.int32, (8, 128), 1)
    meta = jnp.zeros((8, 128), F32)
    for i in range(4):
        meta = jnp.where((row8 == i) & (lane8 == 0), lists[i].astype(F32), meta)
        meta = jnp.where((row8 == i) & (lane8 == 1), ranks[i].astype(F32), meta)
    small[0, 5:8, 0:768] = jnp.zeros((3, 768), F32)
    small[0, :, 768:896] = meta

    def normalise(slot, half):
        rows = block(slot, half)
        values = xraw[rows, :].astype(F32)
        scale = lax.rsqrt(jnp.mean(values * values, axis=-1, keepdims=True) + EPSILON)
        xn[rows, :] = (values * scale * ngain[...]).astype(BF16)

    xraw[0:16, :] = hin[...]
    normalise(0, 0)

    def shared(slot):
        for h in range(2):
            shares[slot, h].wait_recv()
        normalise(slot, 1)

    def gate_tile(first, rows, tile, width):
        x = xn[pl.ds(first, rows), :]
        gate = jnp.dot(x, wg[:, pl.ds(tile, width)], preferred_element_type=F32)
        up = jnp.dot(x, wu[:, pl.ds(tile, width)], preferred_element_type=F32)
        hid[pl.ds(first, rows), pl.ds(tile, width)] = (gate * jax.nn.sigmoid(gate) * up).astype(BF16)

    def hidden_rows(first, rows, width):
        whole = width // 256

        def body(i, carry):
            gate_tile(first, rows, pl.multiple_of(i * 256, 256), 256)
            return carry

        lax.fori_loop(0, whole, body, 0)
        if width % 256:
            gate_tile(first, rows, whole * 256, width % 256)

    units = wg.shape[1]
    for step in range(4):
        for k in range(2):
            for to_right in (True, False):
                h = k if to_right else 1 - k
                if step == 3 and k == 1:
                    continue
                hops[step, h, to_right].wait_recv()
                slot = 7 if step == 3 else (2 * step + 1 if to_right else 2 * step + 2)
                if step < 2 or (step == 2 and k == 0):
                    hops[step + 1, h, to_right] = go(hop(step + 1, h, to_right))
                shares[slot, h] = go(share(slot, h))
        if step == 0:
            shared(0)
            normalise(1, 0)
            normalise(2, 0)
        elif step == 1:
            shared(1)
            shared(2)
            normalise(3, 0)
            normalise(4, 0)
            shared(3)
            shared(4)
            for copy in loads[:8]:
                copy.wait()
        elif step == 2:
            normalise(5, 0)
            normalise(6, 0)
            shared(5)
            shared(6)
    hidden_rows(0, FIRST, units)
    normalise(7, 0)
    shared(7)

    small_copies = {}
    for rel in range(1, CHIPS):
        dst = slot_of(8 - rel)
        small_copies[8 - rel] = go(remote(small.at[0], small.at[2 * dst], sm_s.at[rel], sm_r.at[8 - rel], plane(rel)))
    small_shares = {0: go(remote(small.at[0], small.at[1], sms_s.at[0], sms_r.at[0], sibling))}

    hidden_rows(FIRST, 256 - FIRST, units)

    for rel in range(1, CHIPS):
        small_copies[rel].wait_recv()
        slot = slot_of(rel)
        small_shares[slot] = go(remote(small.at[2 * slot], small.at[2 * slot + 1], sms_s.at[slot], sms_r.at[slot], sibling))

    doc = lax.broadcasted_iota(jnp.int32, (64, 256), 0)
    token = lax.broadcasted_iota(jnp.int32, (64, 256), 1)
    place = (slot_vec((doc & 31) >> 2, p) * 2 + (doc >> 5)) * 4 + (doc & 3)
    pool = jnp.where((token >> 2) == place, 0.25, 0.0).astype(BF16)
    pooled_hidden = jnp.dot(pool, hid[...], preferred_element_type=F32).astype(BF16)
    for copy in loads[8:]:
        copy.wait()

    def columns(rel):
        return pl.ds(pl.multiple_of(chip_at((p + rel) % CHIPS) * COLS, 128), COLS)

    sibs = {}

    def down(rel):
        mixed = jnp.dot(pooled_hidden, wd[:, columns(rel)], preferred_element_type=F32)
        part[rel] = mixed[0:32]
        sib_out[rel] = mixed[32:64]
        sibs[rel] = go(remote(sib_out.at[rel], sib_in.at[rel], sb_s.at[rel], sb_r.at[rel], sibling))

    def mine(rel):
        sibs[rel].wait_recv()
        return part[rel] + sib_in[rel]

    rights, lefts = {}, {}

    def send_right(step):
        total = mine(4 - step)
        if step:
            rights[step - 1].wait_recv()
            total = total + rs_r_in[step - 1].astype(F32)
        rs_r_out[step] = total.astype(BF16)
        rights[step] = go(remote(rs_r_out.at[step], rs_r_in.at[step], rr_s.at[step], rr_r.at[step], right))

    def send_left(step):
        total = mine(5 + step)
        if step:
            lefts[step - 1].wait_recv()
            total = total + rs_l_in[step - 1].astype(F32)
        rs_l_out[step] = total.astype(BF16)
        lefts[step] = go(remote(rs_l_out.at[step], rs_l_in.at[step], rl_s.at[step], rl_r.at[step], left))

    down(4)
    down(5)
    send_right(0)
    send_left(0)
    down(3)
    down(6)
    send_right(1)
    send_left(1)
    down(2)
    down(7)
    send_right(2)
    send_left(2)
    down(1)
    down(0)
    own_cols = columns(0)
    pooled_in = jnp.dot(pool[0:32], xraw[:, own_cols], preferred_element_type=F32)
    send_right(3)

    for slot in range(CHIPS):
        small_shares[slot].wait_recv()
    table = small[:, :, 0:768].reshape(128, 768)
    metas = small[:, :, 768:896].reshape(128, 128)
    row = lax.broadcasted_iota(jnp.int32, (128, 128), 0)
    lane = lax.broadcasted_iota(jnp.int32, (128, 128), 1)
    list_c = jnp.broadcast_to(metas[:, 0:1], (128, 128))
    rank_c = metas[:, 1:2]
    list_r = list_c.T
    doc_c = (row & 7) < 4
    doc_r = (lane & 7) < 4

    def query_place(list_f):
        ids = list_f.astype(jnp.int32)
        half = (ids & 1) ^ c
        return (slot_vec(ids >> 1, p) * 2 + half) * 8 + 4

    highest = lax.Precision.HIGHEST
    grams = lax.dot_general(table, table, (((1,), (1,)), ((), ())), precision=highest, preferred_element_type=F32)
    chosen_hot = jnp.where(doc_c & (lane == query_place(list_c)), 1.0, 0.0)
    root = math.sqrt(768)
    score_c = jnp.broadcast_to(jnp.sum(grams * chosen_hot, axis=1, keepdims=True) / root, (128, 128))
    same = doc_c & doc_r & (list_c == list_r)
    pair = jnp.where(same & (row != lane), 1.0, 0.0)
    sig = jax.nn.sigmoid((score_c.T - score_c) / SOFTMAX_HEAT)
    approx = 1.0 + jnp.sum(pair * sig, axis=1, keepdims=True)
    ln2 = math.log(2.0)
    gains = ln2 / jnp.log(2.0 + rank_c)
    gains_b = jnp.broadcast_to(gains * gains, (128, 128))
    ideal = jnp.sum(jnp.where(same, gains_b.T, 0.0), axis=1, keepdims=True)
    ideal = jnp.where(ideal > 0.0, ideal, 1.0)
    log_a = jnp.log(1.0 + approx) / ln2
    weight = 768.0 * gains / (ideal * log_a * log_a * (1.0 + approx) * ln2)
    weight_b = jnp.broadcast_to(weight, (128, 128))
    pull = pair * sig * (1.0 - sig) / SOFTMAX_HEAT
    grad_c = jnp.broadcast_to(jnp.sum(pull * (weight_b.T - weight_b), axis=1, keepdims=True), (128, 128))
    gvec[...] = grad_c
    hot8 = chosen_hot[0:8]
    chosen = jnp.dot(hot8, table, precision=highest, preferred_element_type=F32)
    grad_r = jnp.where(doc_r & (list_r == t.astype(F32)), grad_c.T, 0.0)[0:8]
    out_query[...] = jnp.dot(grad_r, table, precision=highest, preferred_element_type=F32)[0:1] / root
    in_list = doc_c & (list_c == t.astype(F32))
    earned = jnp.sum(jnp.where(in_list, gains / log_a, 0.0), axis=0, keepdims=True)
    best = jnp.sum(jnp.where(in_list, gains_b, 0.0), axis=0, keepdims=True)
    out_loss[...] = 1.0 - earned / best
    score_part = gvec[0:4, 0:1] * chosen[0:4] / root + small[0, 0:4, 0:768]

    ad_local.wait()
    ad_remote.wait_recv()
    lefts[2].wait_recv()
    rights[3].wait_recv()
    pooled = mine(0) + rs_l_in[2].astype(F32) + rs_r_in[3].astype(F32) + pooled_in
    scaled = pooled * fgain[:, own_cols]
    high = scaled.astype(BF16)
    low = (scaled - high.astype(F32)).astype(BF16)
    both = jnp.dot(jnp.concatenate([high, low], axis=0), ad[...], preferred_element_type=F32)
    product = both[0:32] + both[32:64]
    for q in range(CHIPS):
        fin_out[q, :, 0:COLS] = pooled[4 * q : 4 * q + 4]
        fin_out[q, :, COLS:1408] = product[4 * q : 4 * q + 4]
    finals = []
    for rel in range(1, CHIPS):
        finals.append(
            go(remote(fin_out.at[chip_at((p + rel) % CHIPS)], fin.at[chip], fi_s.at[rel], fi_r.at[8 - rel], plane(rel)))
        )
    fin[chip] = fin_out[chip]
    for copy in finals:
        copy.wait_recv()
    rows = jnp.concatenate([fin[q, :, 0:COLS] for q in range(CHIPS)], axis=1)
    scale = lax.rsqrt(jnp.mean(rows * rows, axis=-1, keepdims=True) + EPSILON)
    out_rows[...] = (rows * scale * fgain[...]).astype(BF16)
    target = fin[0, :, COLS:1408]
    for q in range(1, CHIPS):
        target = target + fin[q, :, COLS:1408]
    out_grad[...] = score_part - target * scale
    for copy in sent:
        copy.wait_send()


def fused(hidden_in, norm_gain, w_gate, w_up, w_down, final_gain, adapter, student_rows, queries, doc_list, teacher_rank):
    units = w_gate.shape[1]
    dma = pltpu.SemaphoreType.DMA
    vmem = pl.BlockSpec(memory_space=pltpu.VMEM)
    smem = pl.BlockSpec(memory_space=pltpu.SMEM)
    hbm = pl.BlockSpec(memory_space=pl.ANY)
    rows, grad, query, loss = pl.pallas_call(
        kernel,
        out_shape=(
            jax.ShapeDtypeStruct((4, 5120), BF16),
            jax.ShapeDtypeStruct((4, 768), F32),
            jax.ShapeDtypeStruct((1, 768), F32),
            jax.ShapeDtypeStruct((1, 128), F32),
        ),
        in_specs=[vmem, vmem, hbm, hbm, hbm, vmem, hbm, vmem, vmem, smem, smem],
        out_specs=(vmem, vmem, vmem, vmem),
        scratch_shapes=[
            pltpu.VMEM((256, 5120), BF16),
            pltpu.VMEM((256, 5120), BF16),
            pltpu.VMEM((5120, units), BF16),
            pltpu.VMEM((5120, units), BF16),
            pltpu.VMEM((units, 5120), BF16),
            pltpu.VMEM((640, 768), BF16),
            pltpu.VMEM((256, units), BF16),
            pltpu.VMEM((CHIPS, 32, COLS), F32),
            pltpu.VMEM((CHIPS, 32, COLS), F32),
            pltpu.VMEM((CHIPS, 32, COLS), F32),
            pltpu.VMEM((4, 32, COLS), BF16),
            pltpu.VMEM((4, 32, COLS), BF16),
            pltpu.VMEM((3, 32, COLS), BF16),
            pltpu.VMEM((3, 32, COLS), BF16),
            pltpu.VMEM((CHIPS, 4, 1408), F32),
            pltpu.VMEM((CHIPS, 4, 1408), F32),
            pltpu.VMEM((16, 8, 896), F32),
            pltpu.VMEM((128, 128), F32),
            dma((3, 4)),
            dma((4, 2)),
            dma((4, 2)),
            dma((4, 2)),
            dma((4, 2)),
            dma((8, 2)),
            dma((8, 2)),
            dma((3,)),
            dma((8,)),
            dma((8,)),
            dma((8,)),
            dma((8,)),
            dma((8,)),
            dma((8,)),
            dma((4,)),
            dma((4,)),
            dma((3,)),
            dma((3,)),
            dma((8,)),
            dma((8,)),
        ],
        compiler_params=pltpu.CompilerParams(
            collective_id=0, has_side_effects=True, vmem_limit_bytes=58 * 1024 * 1024
        ),
        cost_estimate=pl.CostEstimate(flops=8_000_000_000, bytes_accessed=34_000_000, transcendentals=300_000),
    )(
        hidden_in, norm_gain[None, :], w_gate, w_up, w_down, final_gain[None, :], adapter,
        student_rows, queries, doc_list, teacher_rank,
    )
    return rows, grad, query, loss[0, 0:1]


def solution(mesh):
    placed = (
        P(("groups", "tensor"), None),
        P(),
        P(None, "tensor"),
        P(None, "tensor"),
        P("tensor", None),
        P(),
        P("tensor", None),
        P(("groups", "tensor"), None),
        P(("groups", "tensor"), None),
        P(("groups", "tensor")),
        P(("groups", "tensor")),
    )
    return jax.shard_map(
        fused if mesh.shape["tensor"] == 2 * CHIPS else local,
        mesh=mesh,
        in_specs=placed,
        out_specs=(
            P(("groups", "tensor"), None),
            P(("groups", "tensor"), None),
            P(("groups", "tensor"), None),
            P(("groups", "tensor")),
        ),
        check_vma=False,
    )
```

```python
import math

import jax
import jax.numpy as jnp
from jax import lax
from jax.experimental import pallas as pl
from jax.experimental.pallas import tpu as pltpu
from jax.sharding import PartitionSpec as P

SEQ = 4


EPSILON = 1e-06
SOFTMAX_HEAT = 0.5


def list_losses_of(score_values, member, rank_f):
    pairwise_terms = jnp.dot(member, member.T, precision=lax.Precision.HIGHEST)
    pairwise_terms = pairwise_terms * (
        1.0 - jnp.eye(score_values.shape[0], dtype=score_values.dtype)
    )
    outranked_count = pairwise_terms * jax.nn.sigmoid(
        (score_values[None, :] - score_values[:, None]) / SOFTMAX_HEAT
    )
    approx_rank = 1.0 + jnp.sum(outranked_count, axis=1)
    gains = 1.0 / jnp.log2(2.0 + rank_f)
    earned = jnp.dot(member.T, gains / jnp.log2(1.0 + approx_rank), precision=lax.Precision.HIGHEST)
    ideal = jnp.dot(member.T, gains * gains, precision=lax.Precision.HIGHEST)
    return 1.0 - earned / ideal


def local(
    hidden_in,
    norm_gain,
    w_gate,
    w_up,
    w_down,
    final_gain,
    adapter,
    student_rows,
    queries,
    doc_list,
    teacher_rank,
):
    list_entries = lax.axis_size("tensor")
    my_index = lax.axis_index("tensor")
    tokens_f = hidden_in.astype(jnp.float32)
    normed = (
        tokens_f
        * lax.rsqrt(jnp.mean(tokens_f * tokens_f, axis=-1, keepdims=True) + EPSILON)
        * norm_gain
    ).astype(jnp.bfloat16)
    shard_rows = lax.all_gather(normed, "tensor", axis=0, tiled=True)
    gate_out = jnp.dot(shard_rows, w_gate, preferred_element_type=jnp.float32)
    up_out = jnp.dot(shard_rows, w_up, preferred_element_type=jnp.float32)
    hidden = (jax.nn.silu(gate_out) * up_out).astype(jnp.bfloat16)
    doc_rows = hidden_in.shape[0] // SEQ
    mixed = jnp.dot(hidden, w_down, preferred_element_type=jnp.float32)
    pooled_mix = lax.psum_scatter(
        mixed.reshape(lax.axis_size("tensor") * doc_rows, SEQ, mixed.shape[1]).mean(axis=1),
        "tensor",
        scatter_dimension=0,
        tiled=True,
    )
    pooled = pooled_mix + tokens_f.reshape(doc_rows, SEQ, tokens_f.shape[1]).mean(axis=1)
    normed_rows = (
        pooled * lax.rsqrt(jnp.mean(pooled * pooled, axis=-1, keepdims=True) + EPSILON) * final_gain
    )
    teacher_rows = normed_rows.astype(jnp.bfloat16)
    student_width = adapter.shape[1]
    target = jnp.dot(
        teacher_rows,
        lax.all_gather(adapter, "tensor", axis=0, tiled=True),
        preferred_element_type=jnp.float32,
    )
    rows_f = student_rows.astype(jnp.float32)
    residual = rows_f - target
    scale_root = math.sqrt(student_width)
    list_ids = jnp.arange(list_entries, dtype=jnp.int32)
    own_member = doc_list[:, None] == list_ids[None, :]
    query_all = lax.all_gather(queries, "tensor", axis=0, tiled=True)
    own_onehot = own_member.astype(jnp.float32)
    chosen = jnp.dot(own_onehot, query_all, precision=lax.Precision.HIGHEST)
    own_scores = jnp.sum(rows_f * chosen, axis=1) / scale_root
    all_scores = lax.all_gather(own_scores, "tensor", axis=0, tiled=True)
    all_lists, all_ranks = (
        lax.all_gather(doc_list, "tensor", axis=0, tiled=True),
        lax.all_gather(teacher_rank, "tensor", axis=0, tiled=True),
    )
    member = (all_lists[:, None] == list_ids[None, :]).astype(jnp.float32)
    rank_f = all_ranks.astype(jnp.float32)
    per_list, pullback = jax.vjp(lambda values: list_losses_of(values, member, rank_f), all_scores)
    score_grad = pullback(jnp.full(per_list.shape, float(student_width), jnp.float32))[0]
    own_grad = lax.dynamic_slice_in_dim(score_grad, my_index * doc_rows, doc_rows, 0)
    grad_rows = own_grad[:, None] * chosen / scale_root + residual
    query_terms = (
        jnp.dot(own_onehot.T, own_grad[:, None] * rows_f, precision=lax.Precision.HIGHEST)
        / scale_root
    )
    grad_queries = lax.psum_scatter(query_terms, "tensor", scatter_dimension=0, tiled=True)
    own_losses = lax.dynamic_slice_in_dim(per_list, my_index, 1, 0)
    return (teacher_rows, grad_rows, grad_queries, own_losses)


CHIPS = 8
COLS = 640
HALF = 2560
FIRST = 160
F32 = jnp.float32
BF16 = jnp.bfloat16


def chip_at(pos):
    y = pos // 4
    return 2 * (pos + y * (7 - 2 * pos)) + y


def pos_of(chip):
    y = chip % 2
    z = chip // 2
    return z + y * (7 - 2 * z)


def slot_of(rel):
    return 2 * rel if rel < 4 else 15 - 2 * rel


def slot_vec(chip, p):
    y = chip & 1
    z = chip >> 1
    rel = (z + y * (7 - 2 * z) - p + 8) & 7
    return jnp.where(rel < 4, 2 * rel, 15 - 2 * rel)


def kernel(
    hin, ngain, wg_hbm, wu_hbm, wd_hbm, fgain, ad_hbm, student, query, lists, ranks,
    out_rows, out_grad, out_query, out_loss,
    xraw, xn, wg, wu, wd, ad, hid, part, sib_out, sib_in, rs_r_out, rs_r_in, rs_l_out, rs_l_in,
    fin_out, fin, small, gvec,
    w_sem, ag_rs, ag_rr, ag_ls, ag_lr, ag_ss, ag_sr, ad_sem, sm_s, sm_r, sms_s, sms_r,
    sb_s, sb_r, rr_s, rr_r, rl_s, rl_r, fi_s, fi_r,
):
    t = lax.axis_index("tensor")
    c = t % 2
    chip = t // 2
    p = pos_of(chip)

    def plane(rel):
        return chip_at((p + rel) % CHIPS) * 2 + c

    right, left, sibling = plane(1), plane(7), chip * 2 + (1 - c)
    sent = []

    def remote(src, dst, ssem, rsem, dev):
        return pltpu.make_async_remote_copy(
            src_ref=src, dst_ref=dst, send_sem=ssem, recv_sem=rsem,
            device_id={"tensor": dev}, device_id_type=pl.DeviceIdType.MESH,
        )

    def go(copy):
        copy.start()
        sent.append(copy)
        return copy

    barrier = pltpu.get_barrier_semaphore()
    for rel in range(1, CHIPS):
        pl.semaphore_signal(barrier, inc=1, device_id={"tensor": plane(rel)}, device_id_type=pl.DeviceIdType.MESH)
    pl.semaphore_signal(barrier, inc=1, device_id={"tensor": sibling}, device_id_type=pl.DeviceIdType.MESH)

    units = wg.shape[0]
    tiles = [(at, min(256, units - at)) for at in range(0, units, 256)]
    loads = {}
    for i, (src, dst) in enumerate(((wg_hbm, wg), (wu_hbm, wu), (wd_hbm, wd))):
        for j, tile in enumerate(tiles):
            loads[i, j] = pltpu.make_async_copy(src.at[pl.ds(*tile)], dst.at[pl.ds(*tile)], w_sem.at[i, j])
    for j in range(len(tiles)):
        loads[0, j].start()
        loads[1, j].start()
    for j in range(len(tiles)):
        loads[2, j].start()
    ad_rows = pl.ds(pl.multiple_of(c * 320, 64), 320)
    ad_local = pltpu.make_async_copy(ad_hbm, ad.at[ad_rows], ad_sem.at[0])
    ad_local.start()
    pl.semaphore_wait(barrier, CHIPS)

    def block(slot, half):
        return pl.ds((slot * 2 + half) * 16, 16)

    def cols(h):
        return pl.ds(h * HALF, HALF)

    def hop(step, h, to_right):
        if to_right:
            src_slot = 0 if step == 0 else 2 * step - 1
            dst_slot = 2 * step + 1
            ssem, rsem, dev = ag_rs.at[step, h], ag_rr.at[step, h], right
        else:
            src_slot = 2 * step
            dst_slot = 2 * step + 2 if step < 3 else 7
            ssem, rsem, dev = ag_ls.at[step, h], ag_lr.at[step, h], left
        src = hin.at[:, cols(h)] if step == 0 else xraw.at[block(src_slot, 0), cols(h)]
        return remote(src, xraw.at[block(dst_slot, 0), cols(h)], ssem, rsem, dev)

    def share(slot, h):
        src = hin.at[:, cols(h)] if slot == 0 else xraw.at[block(slot, 0), cols(h)]
        return remote(src, xraw.at[block(slot, 1), cols(h)], ag_ss.at[slot, h], ag_sr.at[slot, h], sibling)

    hops = {}
    shares = {}
    for h in range(2):
        hops[0, h, True] = go(hop(0, h, True))
        hops[0, h, False] = go(hop(0, 1 - h, False))
    hops[0, 0, False], hops[0, 1, False] = hops[0, 1, False], hops[0, 0, False]
    for h in range(2):
        shares[0, h] = go(share(0, h))
    ad_remote = go(remote(ad_hbm, ad.at[ad_rows], ad_sem.at[1], ad_sem.at[2], sibling))

    small[0, 0:4, 0:768] = student[...].astype(F32)
    small[0, 4:5, 0:768] = query[...]
    row8 = lax.broadcasted_iota(jnp.int32, (8, 128), 0)
    lane8 = lax.broadcasted_iota(jnp.int32, (8, 128), 1)
    meta = jnp.zeros((8, 128), F32)
    for i in range(4):
        meta = jnp.where((row8 == i) & (lane8 == 0), lists[i].astype(F32), meta)
        meta = jnp.where((row8 == i) & (lane8 == 1), ranks[i].astype(F32), meta)
    small[0, 5:8, 0:768] = jnp.zeros((3, 768), F32)
    small[0, :, 768:896] = meta

    def normalise(slot, half):
        rows = block(slot, half)
        values = xraw[rows, :].astype(F32)
        scale = lax.rsqrt(jnp.mean(values * values, axis=-1, keepdims=True) + EPSILON)
        xn[rows, :] = (values * scale * ngain[...]).astype(BF16)

    xraw[0:16, :] = hin[...]
    normalise(0, 0)

    def shared(slot):
        for h in range(2):
            shares[slot, h].wait_recv()
        normalise(slot, 1)

    def gate_tile(first, rows, at, width):
        x = xn[pl.ds(first, rows), :]
        dims = (((1,), (1,)), ((), ()))
        gate = lax.dot_general(x, wg[pl.ds(at, width), :], dims, preferred_element_type=F32)
        up = lax.dot_general(x, wu[pl.ds(at, width), :], dims, preferred_element_type=F32)
        hid[pl.ds(first, rows), pl.ds(at, width)] = (gate * jax.nn.sigmoid(gate) * up).astype(BF16)

    def early(*which):
        for j in which:
            if j < len(tiles):
                loads[0, j].wait()
                loads[1, j].wait()
                gate_tile(0, FIRST, *tiles[j])

    def hidden_rows(first, rows):
        whole = units // 256

        def body(i, carry):
            gate_tile(first, rows, pl.multiple_of(i * 256, 256), 256)
            return carry

        lax.fori_loop(0, whole, body, 0)
        if units % 256:
            gate_tile(first, rows, whole * 256, units % 256)

    for step in range(4):
        for k in range(2):
            for to_right in (True, False):
                h = k if to_right else 1 - k
                if step == 3 and k == 1:
                    continue
                hops[step, h, to_right].wait_recv()
                slot = 7 if step == 3 else (2 * step + 1 if to_right else 2 * step + 2)
                if step < 2 or (step == 2 and k == 0):
                    hops[step + 1, h, to_right] = go(hop(step + 1, h, to_right))
                shares[slot, h] = go(share(slot, h))
            if step == 2 and k == 0:
                early(1, 2)
        if step == 0:
            shared(0)
            normalise(1, 0)
            normalise(2, 0)
        elif step == 1:
            shared(1)
            shared(2)
            normalise(3, 0)
            normalise(4, 0)
            shared(3)
            shared(4)
            early(0)
        elif step == 2:
            normalise(5, 0)
            normalise(6, 0)
            early(3)
            shared(5)
            shared(6)
    early(*range(4, len(tiles)))
    normalise(7, 0)
    shared(7)

    small_copies = {}
    for rel in range(1, CHIPS):
        dst = slot_of(8 - rel)
        small_copies[8 - rel] = go(remote(small.at[0], small.at[2 * dst], sm_s.at[rel], sm_r.at[8 - rel], plane(rel)))
    small_shares = {0: go(remote(small.at[0], small.at[1], sms_s.at[0], sms_r.at[0], sibling))}

    hidden_rows(FIRST, 256 - FIRST)

    for rel in range(1, CHIPS):
        small_copies[rel].wait_recv()
        slot = slot_of(rel)
        small_shares[slot] = go(remote(small.at[2 * slot], small.at[2 * slot + 1], sms_s.at[slot], sms_r.at[slot], sibling))

    doc = lax.broadcasted_iota(jnp.int32, (64, 256), 0)
    token = lax.broadcasted_iota(jnp.int32, (64, 256), 1)
    place = (slot_vec((doc & 31) >> 2, p) * 2 + (doc >> 5)) * 4 + (doc & 3)
    pool = jnp.where((token >> 2) == place, 0.25, 0.0).astype(BF16)
    pooled_hidden = jnp.dot(pool, hid[...], preferred_element_type=F32).astype(BF16)
    for j in range(len(tiles)):
        loads[2, j].wait()

    def columns(rel):
        return pl.ds(pl.multiple_of(chip_at((p + rel) % CHIPS) * COLS, 128), COLS)

    sibs = {}

    def down(rel):
        mixed = jnp.dot(pooled_hidden, wd[:, columns(rel)], preferred_element_type=F32)
        part[rel] = mixed[0:32]
        sib_out[rel] = mixed[32:64]
        sibs[rel] = go(remote(sib_out.at[rel], sib_in.at[rel], sb_s.at[rel], sb_r.at[rel], sibling))

    def mine(rel):
        sibs[rel].wait_recv()
        return part[rel] + sib_in[rel]

    rights, lefts = {}, {}

    def send_right(step):
        total = mine(4 - step)
        if step:
            rights[step - 1].wait_recv()
            total = total + rs_r_in[step - 1].astype(F32)
        rs_r_out[step] = total.astype(BF16)
        rights[step] = go(remote(rs_r_out.at[step], rs_r_in.at[step], rr_s.at[step], rr_r.at[step], right))

    def send_left(step):
        total = mine(5 + step)
        if step:
            lefts[step - 1].wait_recv()
            total = total + rs_l_in[step - 1].astype(F32)
        rs_l_out[step] = total.astype(BF16)
        lefts[step] = go(remote(rs_l_out.at[step], rs_l_in.at[step], rl_s.at[step], rl_r.at[step], left))

    down(4)
    down(5)
    send_right(0)
    send_left(0)
    down(3)
    down(6)

    for slot in range(CHIPS):
        small_shares[slot].wait_recv()
    table = small[:, :, 0:768].reshape(128, 768)
    metas = small[:, :, 768:896].reshape(128, 128)
    row = lax.broadcasted_iota(jnp.int32, (128, 128), 0)
    lane = lax.broadcasted_iota(jnp.int32, (128, 128), 1)
    list_c = jnp.broadcast_to(metas[:, 0:1], (128, 128))
    rank_c = metas[:, 1:2]
    list_r = list_c.T
    doc_c = (row & 7) < 4
    doc_r = (lane & 7) < 4

    def query_place(list_f):
        ids = list_f.astype(jnp.int32)
        half = (ids & 1) ^ c
        return (slot_vec(ids >> 1, p) * 2 + half) * 8 + 4

    highest = lax.Precision.HIGHEST
    grams = lax.dot_general(table, table, (((1,), (1,)), ((), ())), precision=highest, preferred_element_type=F32)

    send_right(1)
    send_left(1)
    down(2)
    down(7)

    chosen_hot = jnp.where(doc_c & (lane == query_place(list_c)), 1.0, 0.0)
    root = math.sqrt(768)
    score_c = jnp.broadcast_to(jnp.sum(grams * chosen_hot, axis=1, keepdims=True) / root, (128, 128))
    same = doc_c & doc_r & (list_c == list_r)
    pair = jnp.where(same & (row != lane), 1.0, 0.0)
    sig = jax.nn.sigmoid((score_c.T - score_c) / SOFTMAX_HEAT)
    approx = 1.0 + jnp.sum(pair * sig, axis=1, keepdims=True)
    ln2 = math.log(2.0)
    gains = ln2 / jnp.log(2.0 + rank_c)
    gains_b = jnp.broadcast_to(gains * gains, (128, 128))
    ideal = jnp.sum(jnp.where(same, gains_b.T, 0.0), axis=1, keepdims=True)
    ideal = jnp.where(ideal > 0.0, ideal, 1.0)
    log_a = jnp.log(1.0 + approx) / ln2
    weight = 768.0 * gains / (ideal * log_a * log_a * (1.0 + approx) * ln2)
    weight_b = jnp.broadcast_to(weight, (128, 128))
    pull = pair * sig * (1.0 - sig) / SOFTMAX_HEAT
    grad_c = jnp.broadcast_to(jnp.sum(pull * (weight_b.T - weight_b), axis=1, keepdims=True), (128, 128))
    gvec[...] = grad_c

    send_right(2)
    send_left(2)
    down(1)
    down(0)
    own_cols = columns(0)
    pooled_in = jnp.dot(pool[0:32], xraw[:, own_cols], preferred_element_type=F32)
    hot8 = chosen_hot[0:8]
    chosen = jnp.dot(hot8, table, precision=highest, preferred_element_type=F32)
    grad_r = jnp.where(doc_r & (list_r == t.astype(F32)), grad_c.T, 0.0)[0:8]
    out_query[...] = jnp.dot(grad_r, table, precision=highest, preferred_element_type=F32)[0:1] / root
    in_list = doc_c & (list_c == t.astype(F32))
    earned = jnp.sum(jnp.where(in_list, gains / log_a, 0.0), axis=0, keepdims=True)
    best = jnp.sum(jnp.where(in_list, gains_b, 0.0), axis=0, keepdims=True)
    out_loss[...] = 1.0 - earned / best
    score_part = gvec[0:4, 0:1] * chosen[0:4] / root + small[0, 0:4, 0:768]
    send_right(3)

    ad_local.wait()
    ad_remote.wait_recv()
    lefts[2].wait_recv()
    rights[3].wait_recv()
    pooled = mine(0) + rs_l_in[2].astype(F32) + rs_r_in[3].astype(F32) + pooled_in
    scaled = pooled * fgain[:, own_cols]
    high = scaled.astype(BF16)
    low = (scaled - high.astype(F32)).astype(BF16)
    both = jnp.dot(jnp.concatenate([high, low], axis=0), ad[...], preferred_element_type=F32)
    product = both[0:32] + both[32:64]
    for q in range(CHIPS):
        fin_out[q, :, 0:COLS] = pooled[4 * q : 4 * q + 4]
        fin_out[q, :, COLS:1408] = product[4 * q : 4 * q + 4]
    finals = []
    for rel in range(1, CHIPS):
        finals.append(
            go(remote(fin_out.at[chip_at((p + rel) % CHIPS)], fin.at[chip], fi_s.at[rel], fi_r.at[8 - rel], plane(rel)))
        )
    fin[chip] = fin_out[chip]
    for copy in finals:
        copy.wait_recv()
    rows = jnp.concatenate([fin[q, :, 0:COLS] for q in range(CHIPS)], axis=1)
    scale = lax.rsqrt(jnp.mean(rows * rows, axis=-1, keepdims=True) + EPSILON)
    out_rows[...] = (rows * scale * fgain[...]).astype(BF16)
    target = fin[0, :, COLS:1408]
    for q in range(1, CHIPS):
        target = target + fin[q, :, COLS:1408]
    out_grad[...] = score_part - target * scale
    for copy in sent:
        copy.wait_send()


def hand_over(rows, grad, query, loss, out_rows, out_grad, out_query, out_loss):
    out_rows[...] = rows[...]
    out_grad[...] = grad[...]
    out_query[...] = query[...]
    out_loss[0] = loss[0, 0]


def fused(hidden_in, norm_gain, w_gate, w_up, w_down, final_gain, adapter, student_rows, queries, doc_list, teacher_rank):
    units = w_gate.shape[1]
    dma = pltpu.SemaphoreType.DMA
    vmem = pl.BlockSpec(memory_space=pltpu.VMEM)
    smem = pl.BlockSpec(memory_space=pltpu.SMEM)
    hbm = pl.BlockSpec(memory_space=pl.ANY)
    rows, grad, query, loss = pl.pallas_call(
        kernel,
        out_shape=(
            jax.ShapeDtypeStruct((4, 5120), BF16),
            jax.ShapeDtypeStruct((4, 768), F32),
            jax.ShapeDtypeStruct((1, 768), F32),
            jax.ShapeDtypeStruct((1, 128), F32),
        ),
        in_specs=[vmem, vmem, hbm, hbm, hbm, vmem, hbm, vmem, vmem, smem, smem],
        out_specs=(vmem, vmem, vmem, vmem),
        scratch_shapes=[
            pltpu.VMEM((256, 5120), BF16),
            pltpu.VMEM((256, 5120), BF16),
            pltpu.VMEM((units, 5120), BF16),
            pltpu.VMEM((units, 5120), BF16),
            pltpu.VMEM((units, 5120), BF16),
            pltpu.VMEM((640, 768), BF16),
            pltpu.VMEM((256, units), BF16),
            pltpu.VMEM((CHIPS, 32, COLS), F32),
            pltpu.VMEM((CHIPS, 32, COLS), F32),
            pltpu.VMEM((CHIPS, 32, COLS), F32),
            pltpu.VMEM((4, 32, COLS), BF16),
            pltpu.VMEM((4, 32, COLS), BF16),
            pltpu.VMEM((3, 32, COLS), BF16),
            pltpu.VMEM((3, 32, COLS), BF16),
            pltpu.VMEM((CHIPS, 4, 1408), F32),
            pltpu.VMEM((CHIPS, 4, 1408), F32),
            pltpu.VMEM((16, 8, 896), F32),
            pltpu.VMEM((128, 128), F32),
            dma((3, pl.cdiv(units, 256))),
            dma((4, 2)),
            dma((4, 2)),
            dma((4, 2)),
            dma((4, 2)),
            dma((8, 2)),
            dma((8, 2)),
            dma((3,)),
            dma((8,)),
            dma((8,)),
            dma((8,)),
            dma((8,)),
            dma((8,)),
            dma((8,)),
            dma((4,)),
            dma((4,)),
            dma((3,)),
            dma((3,)),
            dma((8,)),
            dma((8,)),
        ],
        compiler_params=pltpu.CompilerParams(
            collective_id=0, has_side_effects=True, vmem_limit_bytes=58 * 1024 * 1024
        ),
        cost_estimate=pl.CostEstimate(flops=8_000_000_000, bytes_accessed=34_000_000, transcendentals=300_000),
    )(
        hidden_in, norm_gain[None, :], w_gate.T, w_up.T, w_down, final_gain[None, :], adapter,
        student_rows, queries, doc_list, teacher_rank,
    )
    return pl.pallas_call(
        hand_over,
        out_shape=(
            jax.ShapeDtypeStruct(rows.shape, BF16),
            jax.ShapeDtypeStruct(grad.shape, F32),
            jax.ShapeDtypeStruct(query.shape, F32),
            jax.ShapeDtypeStruct((1,), F32),
        ),
        in_specs=[vmem, vmem, vmem, vmem],
        out_specs=(vmem, vmem, vmem, smem),
    )(rows, grad, query, loss)


def solution(mesh):
    placed = (
        P(("groups", "tensor"), None),
        P(),
        P(None, "tensor"),
        P(None, "tensor"),
        P("tensor", None),
        P(),
        P("tensor", None),
        P(("groups", "tensor"), None),
        P(("groups", "tensor"), None),
        P(("groups", "tensor")),
        P(("groups", "tensor")),
    )
    return jax.shard_map(
        fused if mesh.shape["tensor"] == 2 * CHIPS else local,
        mesh=mesh,
        in_specs=placed,
        out_specs=(
            P(("groups", "tensor"), None),
            P(("groups", "tensor"), None),
            P(("groups", "tensor"), None),
            P(("groups", "tensor")),
        ),
        check_vma=False,
    )
```

```python
import math

import jax
import jax.numpy as jnp
from jax import lax
from jax.experimental import pallas as pl
from jax.experimental.pallas import tpu as pltpu
from jax.sharding import PartitionSpec as P

SEQ = 4


EPSILON = 1e-06
SOFTMAX_HEAT = 0.5


def list_losses_of(score_values, member, rank_f):
    pairwise_terms = jnp.dot(member, member.T, precision=lax.Precision.HIGHEST)
    pairwise_terms = pairwise_terms * (
        1.0 - jnp.eye(score_values.shape[0], dtype=score_values.dtype)
    )
    outranked_count = pairwise_terms * jax.nn.sigmoid(
        (score_values[None, :] - score_values[:, None]) / SOFTMAX_HEAT
    )
    approx_rank = 1.0 + jnp.sum(outranked_count, axis=1)
    gains = 1.0 / jnp.log2(2.0 + rank_f)
    earned = jnp.dot(member.T, gains / jnp.log2(1.0 + approx_rank), precision=lax.Precision.HIGHEST)
    ideal = jnp.dot(member.T, gains * gains, precision=lax.Precision.HIGHEST)
    return 1.0 - earned / ideal


def local(
    hidden_in,
    norm_gain,
    w_gate,
    w_up,
    w_down,
    final_gain,
    adapter,
    student_rows,
    queries,
    doc_list,
    teacher_rank,
):
    list_entries = lax.axis_size("tensor")
    my_index = lax.axis_index("tensor")
    tokens_f = hidden_in.astype(jnp.float32)
    normed = (
        tokens_f
        * lax.rsqrt(jnp.mean(tokens_f * tokens_f, axis=-1, keepdims=True) + EPSILON)
        * norm_gain
    ).astype(jnp.bfloat16)
    shard_rows = lax.all_gather(normed, "tensor", axis=0, tiled=True)
    gate_out = jnp.dot(shard_rows, w_gate, preferred_element_type=jnp.float32)
    up_out = jnp.dot(shard_rows, w_up, preferred_element_type=jnp.float32)
    hidden = (jax.nn.silu(gate_out) * up_out).astype(jnp.bfloat16)
    doc_rows = hidden_in.shape[0] // SEQ
    mixed = jnp.dot(hidden, w_down, preferred_element_type=jnp.float32)
    pooled_mix = lax.psum_scatter(
        mixed.reshape(lax.axis_size("tensor") * doc_rows, SEQ, mixed.shape[1]).mean(axis=1),
        "tensor",
        scatter_dimension=0,
        tiled=True,
    )
    pooled = pooled_mix + tokens_f.reshape(doc_rows, SEQ, tokens_f.shape[1]).mean(axis=1)
    normed_rows = (
        pooled * lax.rsqrt(jnp.mean(pooled * pooled, axis=-1, keepdims=True) + EPSILON) * final_gain
    )
    teacher_rows = normed_rows.astype(jnp.bfloat16)
    student_width = adapter.shape[1]
    target = jnp.dot(
        teacher_rows,
        lax.all_gather(adapter, "tensor", axis=0, tiled=True),
        preferred_element_type=jnp.float32,
    )
    rows_f = student_rows.astype(jnp.float32)
    residual = rows_f - target
    scale_root = math.sqrt(student_width)
    list_ids = jnp.arange(list_entries, dtype=jnp.int32)
    own_member = doc_list[:, None] == list_ids[None, :]
    query_all = lax.all_gather(queries, "tensor", axis=0, tiled=True)
    own_onehot = own_member.astype(jnp.float32)
    chosen = jnp.dot(own_onehot, query_all, precision=lax.Precision.HIGHEST)
    own_scores = jnp.sum(rows_f * chosen, axis=1) / scale_root
    all_scores = lax.all_gather(own_scores, "tensor", axis=0, tiled=True)
    all_lists, all_ranks = (
        lax.all_gather(doc_list, "tensor", axis=0, tiled=True),
        lax.all_gather(teacher_rank, "tensor", axis=0, tiled=True),
    )
    member = (all_lists[:, None] == list_ids[None, :]).astype(jnp.float32)
    rank_f = all_ranks.astype(jnp.float32)
    per_list, pullback = jax.vjp(lambda values: list_losses_of(values, member, rank_f), all_scores)
    score_grad = pullback(jnp.full(per_list.shape, float(student_width), jnp.float32))[0]
    own_grad = lax.dynamic_slice_in_dim(score_grad, my_index * doc_rows, doc_rows, 0)
    grad_rows = own_grad[:, None] * chosen / scale_root + residual
    query_terms = (
        jnp.dot(own_onehot.T, own_grad[:, None] * rows_f, precision=lax.Precision.HIGHEST)
        / scale_root
    )
    grad_queries = lax.psum_scatter(query_terms, "tensor", scatter_dimension=0, tiled=True)
    own_losses = lax.dynamic_slice_in_dim(per_list, my_index, 1, 0)
    return (teacher_rows, grad_rows, grad_queries, own_losses)


CHIPS = 8
COLS = 640
HALF = 2560
FIRST = 160
F32 = jnp.float32
BF16 = jnp.bfloat16


def chip_at(pos):
    y = pos // 4
    return 2 * (pos + y * (7 - 2 * pos)) + y


def pos_of(chip):
    y = chip % 2
    z = chip // 2
    return z + y * (7 - 2 * z)


def slot_of(rel):
    return 2 * rel if rel < 4 else 15 - 2 * rel


def slot_vec(chip, p):
    y = chip & 1
    z = chip >> 1
    rel = (z + y * (7 - 2 * z) - p + 8) & 7
    return jnp.where(rel < 4, 2 * rel, 15 - 2 * rel)


def kernel(
    hin, ngain, wg_hbm, wu_hbm, wd_hbm, fgain, ad_hbm, student, query, lists, ranks,
    out_rows, out_grad, out_query, out_loss,
    xraw, xn, wg, wu, wd, ad, hid, part, sib_out, sib_in, rs_r_out, rs_r_in, rs_l_out, rs_l_in,
    fin_out, fin, small, gvec,
    w_sem, ag_rs, ag_rr, ag_ls, ag_lr, ag_ss, ag_sr, ad_sem, sm_s, sm_r, sms_s, sms_r,
    sb_s, sb_r, rr_s, rr_r, rl_s, rl_r, fi_s, fi_r,
):
    t = lax.axis_index("tensor")
    c = t % 2
    chip = t // 2
    p = pos_of(chip)

    def plane(rel):
        return chip_at((p + rel) % CHIPS) * 2 + c

    right, left, sibling = plane(1), plane(7), chip * 2 + (1 - c)
    sent = []

    def remote(src, dst, ssem, rsem, dev):
        return pltpu.make_async_remote_copy(
            src_ref=src, dst_ref=dst, send_sem=ssem, recv_sem=rsem,
            device_id={"tensor": dev}, device_id_type=pl.DeviceIdType.MESH,
        )

    def go(copy):
        copy.start()
        sent.append(copy)
        return copy

    barrier = pltpu.get_barrier_semaphore()
    for rel in range(1, CHIPS):
        pl.semaphore_signal(barrier, inc=1, device_id={"tensor": plane(rel)}, device_id_type=pl.DeviceIdType.MESH)
    pl.semaphore_signal(barrier, inc=1, device_id={"tensor": sibling}, device_id_type=pl.DeviceIdType.MESH)

    units = wg.shape[0]
    tiles = [(at, min(256, units - at)) for at in range(0, units, 256)]
    loads = {}
    for i, (src, dst) in enumerate(((wg_hbm, wg), (wu_hbm, wu), (wd_hbm, wd))):
        for j, tile in enumerate(tiles):
            loads[i, j] = pltpu.make_async_copy(src.at[pl.ds(*tile)], dst.at[pl.ds(*tile)], w_sem.at[i, j])
    for j in range(len(tiles)):
        loads[0, j].start()
        loads[1, j].start()
    for j in range(len(tiles)):
        loads[2, j].start()
    ad_rows = pl.ds(pl.multiple_of(c * 320, 64), 320)
    ad_local = pltpu.make_async_copy(ad_hbm, ad.at[ad_rows], ad_sem.at[0])
    ad_local.start()
    pl.semaphore_wait(barrier, CHIPS)

    def block(slot, half):
        return pl.ds((slot * 2 + half) * 16, 16)

    def cols(h):
        return pl.ds(h * HALF, HALF)

    def hop(step, h, to_right):
        if to_right:
            src_slot = 0 if step == 0 else 2 * step - 1
            dst_slot = 2 * step + 1
            ssem, rsem, dev = ag_rs.at[step, h], ag_rr.at[step, h], right
        else:
            src_slot = 2 * step
            dst_slot = 2 * step + 2 if step < 3 else 7
            ssem, rsem, dev = ag_ls.at[step, h], ag_lr.at[step, h], left
        src = hin.at[:, cols(h)] if step == 0 else xraw.at[block(src_slot, 0), cols(h)]
        return remote(src, xraw.at[block(dst_slot, 0), cols(h)], ssem, rsem, dev)

    def share(slot, h):
        src = hin.at[:, cols(h)] if slot == 0 else xraw.at[block(slot, 0), cols(h)]
        return remote(src, xraw.at[block(slot, 1), cols(h)], ag_ss.at[slot, h], ag_sr.at[slot, h], sibling)

    hops = {}
    shares = {}
    for h in range(2):
        hops[0, h, True] = go(hop(0, h, True))
        hops[0, h, False] = go(hop(0, 1 - h, False))
    hops[0, 0, False], hops[0, 1, False] = hops[0, 1, False], hops[0, 0, False]
    for h in range(2):
        shares[0, h] = go(share(0, h))
    ad_remote = go(remote(ad_hbm, ad.at[ad_rows], ad_sem.at[1], ad_sem.at[2], sibling))

    small[0, 0:4, 0:768] = student[...].astype(F32)
    small[0, 4:5, 0:768] = query[...]
    row8 = lax.broadcasted_iota(jnp.int32, (8, 128), 0)
    lane8 = lax.broadcasted_iota(jnp.int32, (8, 128), 1)
    meta = jnp.zeros((8, 128), F32)
    for i in range(4):
        meta = jnp.where((row8 == i) & (lane8 == 0), lists[i].astype(F32), meta)
        meta = jnp.where((row8 == i) & (lane8 == 1), ranks[i].astype(F32), meta)
    small[0, 5:8, 0:768] = jnp.zeros((3, 768), F32)
    small[0, :, 768:896] = meta
    small_copies = {}
    for rel in range(1, CHIPS):
        dst = slot_of(8 - rel)
        small_copies[8 - rel] = go(remote(small.at[0], small.at[2 * dst], sm_s.at[rel], sm_r.at[8 - rel], plane(rel)))
    small_shares = {0: go(remote(small.at[0], small.at[1], sms_s.at[0], sms_r.at[0], sibling))}

    def normalise(slot, half):
        rows = block(slot, half)
        values = xraw[rows, :].astype(F32)
        scale = lax.rsqrt(jnp.mean(values * values, axis=-1, keepdims=True) + EPSILON)
        xn[rows, :] = (values * scale * ngain[...]).astype(BF16)

    xraw[0:16, :] = hin[...]
    normalise(0, 0)

    def shared(slot):
        for h in range(2):
            shares[slot, h].wait_recv()
        normalise(slot, 1)

    def gate_tile(first, rows, at, width):
        x = xn[pl.ds(first, rows), :]
        dims = (((1,), (1,)), ((), ()))
        gate = lax.dot_general(x, wg[pl.ds(at, width), :], dims, preferred_element_type=F32)
        up = lax.dot_general(x, wu[pl.ds(at, width), :], dims, preferred_element_type=F32)
        hid[pl.ds(first, rows), pl.ds(at, width)] = (gate * jax.nn.sigmoid(gate) * up).astype(BF16)

    def early(*which):
        for j in which:
            if j < len(tiles):
                loads[0, j].wait()
                loads[1, j].wait()
                gate_tile(0, FIRST, *tiles[j])

    def hidden_rows(first, rows):
        whole = units // 256

        def body(i, carry):
            gate_tile(first, rows, pl.multiple_of(i * 256, 256), 256)
            return carry

        lax.fori_loop(0, whole, body, 0)
        if units % 256:
            gate_tile(first, rows, whole * 256, units % 256)

    for step in range(4):
        for k in range(2):
            for to_right in (True, False):
                h = k if to_right else 1 - k
                if step == 3 and k == 1:
                    continue
                hops[step, h, to_right].wait_recv()
                slot = 7 if step == 3 else (2 * step + 1 if to_right else 2 * step + 2)
                if step < 2 or (step == 2 and k == 0):
                    hops[step + 1, h, to_right] = go(hop(step + 1, h, to_right))
                shares[slot, h] = go(share(slot, h))
            if step == 2 and k == 0:
                early(1, 2)
        if step == 0:
            shared(0)
            normalise(1, 0)
            normalise(2, 0)
        elif step == 1:
            shared(1)
            shared(2)
            normalise(3, 0)
            normalise(4, 0)
            shared(3)
            shared(4)
            early(0)
        elif step == 2:
            normalise(5, 0)
            normalise(6, 0)
            early(3)
            shared(5)
            shared(6)
    early(*range(4, len(tiles)))
    normalise(7, 0)
    shared(7)

    hidden_rows(FIRST, 256 - FIRST)

    for rel in range(1, CHIPS):
        small_copies[rel].wait_recv()
        slot = slot_of(rel)
        small_shares[slot] = go(remote(small.at[2 * slot], small.at[2 * slot + 1], sms_s.at[slot], sms_r.at[slot], sibling))

    doc = lax.broadcasted_iota(jnp.int32, (64, 256), 0)
    token = lax.broadcasted_iota(jnp.int32, (64, 256), 1)
    place = (slot_vec((doc & 31) >> 2, p) * 2 + (doc >> 5)) * 4 + (doc & 3)
    pool = jnp.where((token >> 2) == place, 0.25, 0.0).astype(BF16)
    pooled_hidden = jnp.dot(pool, hid[...], preferred_element_type=F32).astype(BF16)
    for j in range(len(tiles)):
        loads[2, j].wait()

    def columns(rel):
        return pl.ds(pl.multiple_of(chip_at((p + rel) % CHIPS) * COLS, 128), COLS)

    sibs = {}

    def down(rel):
        mixed = jnp.dot(pooled_hidden, wd[:, columns(rel)], preferred_element_type=F32)
        part[rel] = mixed[0:32]
        sib_out[rel] = mixed[32:64]
        sibs[rel] = go(remote(sib_out.at[rel], sib_in.at[rel], sb_s.at[rel], sb_r.at[rel], sibling))

    def mine(rel):
        sibs[rel].wait_recv()
        return part[rel] + sib_in[rel]

    rights, lefts = {}, {}

    def send_right(step):
        total = mine(4 - step)
        if step:
            rights[step - 1].wait_recv()
            total = total + rs_r_in[step - 1].astype(F32)
        rs_r_out[step] = total.astype(BF16)
        rights[step] = go(remote(rs_r_out.at[step], rs_r_in.at[step], rr_s.at[step], rr_r.at[step], right))

    def send_left(step):
        total = mine(5 + step)
        if step:
            lefts[step - 1].wait_recv()
            total = total + rs_l_in[step - 1].astype(F32)
        rs_l_out[step] = total.astype(BF16)
        lefts[step] = go(remote(rs_l_out.at[step], rs_l_in.at[step], rl_s.at[step], rl_r.at[step], left))

    down(4)
    down(5)
    send_right(0)
    send_left(0)
    down(3)
    down(6)

    for slot in range(CHIPS):
        small_shares[slot].wait_recv()
    table = small[:, :, 0:768].reshape(128, 768)
    metas = small[:, :, 768:896].reshape(128, 128)
    row = lax.broadcasted_iota(jnp.int32, (128, 128), 0)
    lane = lax.broadcasted_iota(jnp.int32, (128, 128), 1)
    list_c = jnp.broadcast_to(metas[:, 0:1], (128, 128))
    rank_c = metas[:, 1:2]
    list_r = list_c.T
    doc_c = (row & 7) < 4
    doc_r = (lane & 7) < 4

    def query_place(list_f):
        ids = list_f.astype(jnp.int32)
        half = (ids & 1) ^ c
        return (slot_vec(ids >> 1, p) * 2 + half) * 8 + 4

    highest = lax.Precision.HIGHEST
    grams = lax.dot_general(table, table, (((1,), (1,)), ((), ())), precision=highest, preferred_element_type=F32)

    send_right(1)
    send_left(1)
    down(2)
    down(7)

    chosen_hot = jnp.where(doc_c & (lane == query_place(list_c)), 1.0, 0.0)
    root = math.sqrt(768)
    score_c = jnp.broadcast_to(jnp.sum(grams * chosen_hot, axis=1, keepdims=True) / root, (128, 128))
    same = doc_c & doc_r & (list_c == list_r)
    pair = jnp.where(same & (row != lane), 1.0, 0.0)
    sig = jax.nn.sigmoid((score_c.T - score_c) / SOFTMAX_HEAT)
    approx = 1.0 + jnp.sum(pair * sig, axis=1, keepdims=True)
    ln2 = math.log(2.0)
    gains = ln2 / jnp.log(2.0 + rank_c)
    gains_b = jnp.broadcast_to(gains * gains, (128, 128))
    ideal = jnp.sum(jnp.where(same, gains_b.T, 0.0), axis=1, keepdims=True)
    ideal = jnp.where(ideal > 0.0, ideal, 1.0)
    log_a = jnp.log(1.0 + approx) / ln2
    weight = 768.0 * gains / (ideal * log_a * log_a * (1.0 + approx) * ln2)
    weight_b = jnp.broadcast_to(weight, (128, 128))
    pull = pair * sig * (1.0 - sig) / SOFTMAX_HEAT
    grad_c = jnp.broadcast_to(jnp.sum(pull * (weight_b.T - weight_b), axis=1, keepdims=True), (128, 128))
    gvec[...] = grad_c

    send_right(2)
    send_left(2)
    down(1)
    down(0)
    own_cols = columns(0)
    pooled_in = jnp.dot(pool[0:32], xraw[:, own_cols], preferred_element_type=F32)
    hot8 = chosen_hot[0:8]
    chosen = jnp.dot(hot8, table, precision=highest, preferred_element_type=F32)
    grad_r = jnp.where(doc_r & (list_r == t.astype(F32)), grad_c.T, 0.0)[0:8]
    out_query[...] = jnp.dot(grad_r, table, precision=highest, preferred_element_type=F32)[0:1] / root
    in_list = doc_c & (list_c == t.astype(F32))
    earned = jnp.sum(jnp.where(in_list, gains / log_a, 0.0), axis=0, keepdims=True)
    best = jnp.sum(jnp.where(in_list, gains_b, 0.0), axis=0, keepdims=True)
    out_loss[...] = 1.0 - earned / best
    score_part = gvec[0:4, 0:1] * chosen[0:4] / root + small[0, 0:4, 0:768]
    send_right(3)

    ad_local.wait()
    ad_remote.wait_recv()
    lefts[2].wait_recv()
    rights[3].wait_recv()
    pooled = mine(0) + rs_l_in[2].astype(F32) + rs_r_in[3].astype(F32) + pooled_in
    scaled = pooled * fgain[:, own_cols]
    high = scaled.astype(BF16)
    low = (scaled - high.astype(F32)).astype(BF16)
    both = jnp.dot(jnp.concatenate([high, low], axis=0), ad[...], preferred_element_type=F32)
    product = both[0:32] + both[32:64]
    for q in range(CHIPS):
        fin_out[q, :, 0:COLS] = pooled[4 * q : 4 * q + 4]
        fin_out[q, :, COLS:1408] = product[4 * q : 4 * q + 4]
    finals = []
    for rel in range(1, CHIPS):
        finals.append(
            go(remote(fin_out.at[chip_at((p + rel) % CHIPS)], fin.at[chip], fi_s.at[rel], fi_r.at[8 - rel], plane(rel)))
        )
    fin[chip] = fin_out[chip]
    for copy in finals:
        copy.wait_recv()
    rows = jnp.concatenate([fin[q, :, 0:COLS] for q in range(CHIPS)], axis=1)
    scale = lax.rsqrt(jnp.mean(rows * rows, axis=-1, keepdims=True) + EPSILON)
    out_rows[...] = (rows * scale * fgain[...]).astype(BF16)
    target = fin[0, :, COLS:1408]
    for q in range(1, CHIPS):
        target = target + fin[q, :, COLS:1408]
    out_grad[...] = score_part - target * scale
    for copy in sent:
        copy.wait_send()


def hand_over(rows, grad, query, loss, out_rows, out_grad, out_query, out_loss):
    out_rows[...] = rows[...]
    out_grad[...] = grad[...]
    out_query[...] = query[...]
    out_loss[0] = loss[0, 0]


def fused(hidden_in, norm_gain, w_gate, w_up, w_down, final_gain, adapter, student_rows, queries, doc_list, teacher_rank):
    units = w_gate.shape[1]
    dma = pltpu.SemaphoreType.DMA
    vmem = pl.BlockSpec(memory_space=pltpu.VMEM)
    smem = pl.BlockSpec(memory_space=pltpu.SMEM)
    hbm = pl.BlockSpec(memory_space=pl.ANY)
    rows, grad, query, loss = pl.pallas_call(
        kernel,
        out_shape=(
            jax.ShapeDtypeStruct((4, 5120), BF16),
            jax.ShapeDtypeStruct((4, 768), F32),
            jax.ShapeDtypeStruct((1, 768), F32),
            jax.ShapeDtypeStruct((1, 128), F32),
        ),
        in_specs=[vmem, vmem, hbm, hbm, hbm, vmem, hbm, vmem, vmem, smem, smem],
        out_specs=(vmem, vmem, vmem, vmem),
        scratch_shapes=[
            pltpu.VMEM((256, 5120), BF16),
            pltpu.VMEM((256, 5120), BF16),
            pltpu.VMEM((units, 5120), BF16),
            pltpu.VMEM((units, 5120), BF16),
            pltpu.VMEM((units, 5120), BF16),
            pltpu.VMEM((640, 768), BF16),
            pltpu.VMEM((256, units), BF16),
            pltpu.VMEM((CHIPS, 32, COLS), F32),
            pltpu.VMEM((CHIPS, 32, COLS), F32),
            pltpu.VMEM((CHIPS, 32, COLS), F32),
            pltpu.VMEM((4, 32, COLS), BF16),
            pltpu.VMEM((4, 32, COLS), BF16),
            pltpu.VMEM((3, 32, COLS), BF16),
            pltpu.VMEM((3, 32, COLS), BF16),
            pltpu.VMEM((CHIPS, 4, 1408), F32),
            pltpu.VMEM((CHIPS, 4, 1408), F32),
            pltpu.VMEM((16, 8, 896), F32),
            pltpu.VMEM((128, 128), F32),
            dma((3, pl.cdiv(units, 256))),
            dma((4, 2)),
            dma((4, 2)),
            dma((4, 2)),
            dma((4, 2)),
            dma((8, 2)),
            dma((8, 2)),
            dma((3,)),
            dma((8,)),
            dma((8,)),
            dma((8,)),
            dma((8,)),
            dma((8,)),
            dma((8,)),
            dma((4,)),
            dma((4,)),
            dma((3,)),
            dma((3,)),
            dma((8,)),
            dma((8,)),
        ],
        compiler_params=pltpu.CompilerParams(
            collective_id=0, has_side_effects=True, vmem_limit_bytes=58 * 1024 * 1024
        ),
        cost_estimate=pl.CostEstimate(flops=8_000_000_000, bytes_accessed=34_000_000, transcendentals=300_000),
    )(
        hidden_in, norm_gain[None, :], w_gate.T, w_up.T, w_down, final_gain[None, :], adapter,
        student_rows, queries, doc_list, teacher_rank,
    )
    return pl.pallas_call(
        hand_over,
        out_shape=(
            jax.ShapeDtypeStruct(rows.shape, BF16),
            jax.ShapeDtypeStruct(grad.shape, F32),
            jax.ShapeDtypeStruct(query.shape, F32),
            jax.ShapeDtypeStruct((1,), F32),
        ),
        in_specs=[vmem, vmem, vmem, vmem],
        out_specs=(vmem, vmem, vmem, smem),
    )(rows, grad, query, loss)


def solution(mesh):
    placed = (
        P(("groups", "tensor"), None),
        P(),
        P(None, "tensor"),
        P(None, "tensor"),
        P("tensor", None),
        P(),
        P("tensor", None),
        P(("groups", "tensor"), None),
        P(("groups", "tensor"), None),
        P(("groups", "tensor")),
        P(("groups", "tensor")),
    )
    return jax.shard_map(
        fused if mesh.shape["tensor"] == 2 * CHIPS else local,
        mesh=mesh,
        in_specs=placed,
        out_specs=(
            P(("groups", "tensor"), None),
            P(("groups", "tensor"), None),
            P(("groups", "tensor"), None),
            P(("groups", "tensor")),
        ),
        check_vma=False,
    )
```
